512 devices in a mesh: pp: 16 (over x, z_lo), ep: 32 (over y, z_hi, core).
Axes of the slice: x: 4, y: 8, z: 8 (z_hi: 2, z_lo: 4; z = z_hi * 4 + z_lo), core: 2. Of those that a mesh axis runs over, the one named last changes fastest.
Arguments:
- tokens: bfloat16 [16, 8192, 2048], P('pp', 'ep'), may hold values from -6 to 6
- gain_section: bfloat16 [16, 2048], P('pp'), may hold values from 0.099609375 to 1.8984375
- gate_weight: bfloat16 [16, 32, 2048, 192], P('pp', 'ep'), may hold values from -0.125 to 0.125
- up_weight: bfloat16 [16, 32, 2048, 192], P('pp', 'ep'), may hold values from -0.125 to 0.125
- down_weight: bfloat16 [16, 32, 192, 2048], P('pp', 'ep'), may hold values from -0.15625 to 0.15625
- routes: int32 [16, 8192, 8], P('pp', 'ep'), may hold values from 0 to 127, as said below
- mixing: float32 [16, 8192, 8], P('pp', 'ep'), may hold values from 0.1 to 1
Outputs:
- result: bfloat16 [16, 8192, 2048], P('pp', 'ep')
The draws below stay inside these ranges and needn't reach their ends.
Inputs may be any that keep to these rules, and one draw needn't show every extreme that they name: `routes`: each row names 8 different experts. Within the 256 rows of one device each expert below 4 is named by at most 32 rows; in every section one such expert, drawn from the seed, is named by exactly 32 rows of every device.
All inputs are finite; a program needn't handle non-finite values.
Results may differ from the reference program's by a relative error of at most 0.0017.
Values may be sent and summed in bfloat16 or wider, within the bound.
No kernel may reach another device: no remote copies, remote signals or barrier semaphores. Data moves between devices by JAX's collectives and lax.ppermute only.
A program may use at most 64 MiB of HBM per device.

```python
import math
import jax
import jax.numpy as jnp
from jax import lax

D = 2048
EXPERTS = 128
TOP = 8
SLICES = 8
H_DEV = 192
FF_E = 1536
TOK_DEV = 256
CAP = 32
NPP = 16
WAVE = 4
SEQ = 8192
N_EP = 32


def routes_law(key):
    held = WAVE
    k_hot, k_count, k_rank, k_other = jax.random.split(key, 4)
    hottest = jax.random.randint(k_hot, (NPP, 1, 1), 0, held)
    counts = jax.random.randint(k_count, (NPP, N_EP, held), 2, CAP)
    counts = jnp.where(jnp.arange(held)[None, None, :] == hottest, CAP, counts)
    noise = jax.random.randint(k_rank, (NPP, N_EP, held, TOK_DEV), 0, 2 ** 20)
    keyed = noise * TOK_DEV + jnp.arange(TOK_DEV, dtype=jnp.int32)
    ranks = jnp.argsort(jnp.argsort(keyed, axis=-1), axis=-1)
    member = ranks < counts[..., None]
    member = jnp.transpose(member, (0, 1, 3, 2))
    spare = EXPERTS - held
    scores = jax.random.randint(k_other, (NPP, N_EP, TOK_DEV, spare), 0, 2 ** 16) * EXPERTS + jnp.arange(spare, dtype=jnp.int32)
    others = lax.top_k(scores, TOP)[1].astype(jnp.int32) + held
    labels = jnp.broadcast_to(jnp.arange(held, dtype=jnp.int32), (NPP, N_EP, TOK_DEV, held))
    candidates = jnp.concatenate([labels, others], axis=-1)
    wave_keys = jnp.where(member, labels, labels + 4 * EXPERTS)
    other_keys = jnp.broadcast_to(jnp.arange(TOP, dtype=jnp.int32) + held, (NPP, N_EP, TOK_DEV, TOP))
    order = jnp.argsort(jnp.concatenate([wave_keys, other_keys], axis=-1), axis=-1, stable=True)[..., :TOP]
    picks = jnp.take_along_axis(candidates, order, axis=-1)
    return picks.reshape(NPP, SEQ, TOP).astype(jnp.int32)


def draw_routes(key, part):
    key = jax.random.fold_in(key, 11)
    return routes_law(key)


def levels(rng, extent, pieces, smallest, largest):
    def one(axis_at, blocks):
        steps = jax.random.uniform(jax.random.fold_in(jax.random.fold_in(rng, 6), axis_at), (blocks,), jnp.float32, smallest / len(pieces), largest / len(pieces))
        return jnp.repeat(jnp.exp(steps), extent[axis_at] // blocks).reshape((-1,) + (1,) * (len(extent) - axis_at - 1))

    loudness = one(*pieces[0])
    for cut in pieces[1:]:
        loudness = loudness * one(*cut)
    return loudness


def gaussian(key, dims, spread, bound, cuts=(), kind=jnp.bfloat16):
    drawn = spread * jax.random.normal(key, dims, jnp.float32)
    if cuts:
        drawn = drawn * levels(key, dims, cuts, -0.22, 0.18)
    return jnp.clip(drawn, -bound, bound).astype(kind)


def setup_inputs(seed: int = 0) -> dict:
    streams_of = jax.random.split(jax.random.key(seed), 8)
    tokens = gaussian(streams_of[0], (NPP, SEQ, D), 1.0, 6.0, ((0, 16), (1, 32)))
    gain_section = jnp.clip(1.0 + 0.18 * jax.random.normal(streams_of[1], (NPP, D), jnp.float32), 0.099609375, 1.8984375).astype(jnp.bfloat16)
    gate_weight = gaussian(streams_of[2], (NPP, N_EP, D, H_DEV), D ** -0.5, 0.125, ((0, 16), (1, 32)))
    up_weight = gaussian(streams_of[3], (NPP, N_EP, D, H_DEV), D ** -0.5, 0.125, ((0, 16), (1, 32)))
    down_weight = gaussian(streams_of[4], (NPP, N_EP, H_DEV, D), FF_E ** -0.5, 0.15625, ((0, 16), (1, 32)))
    routes = draw_routes(jax.random.fold_in(streams_of[7], 71), 0)
    mixing = jnp.clip(jnp.exp(math.log(1.0) - 2.3025851 * jax.random.uniform(streams_of[6], (NPP, SEQ, TOP), jnp.float32) ** levels(streams_of[6], (NPP, SEQ, TOP), ((0, 16), (1, 32)), -0.2, 0.2)), 0.1, 1.0)
    return dict(tokens=tokens, gain_section=gain_section, gate_weight=gate_weight, up_weight=up_weight, down_weight=down_weight, routes=routes, mixing=mixing)


EPSILON = 1e-06

def rms_normed(values, gain_row):
    widened = values.astype(jnp.float32)
    scale_row = lax.rsqrt(lax.optimization_barrier(jnp.mean(widened * widened, axis=-1, keepdims=True)) + EPSILON)
    return (widened * scale_row * gain_row.astype(jnp.float32)).astype(jnp.bfloat16)

def expert_block(token_rows, gate_mat, up_mat, down_mat):
    gate_proj = jnp.dot(token_rows, gate_mat, preferred_element_type=jnp.float32)
    up_proj = jnp.dot(token_rows, up_mat, preferred_element_type=jnp.float32)
    hidden = (jax.nn.silu(gate_proj) * up_proj).astype(jnp.bfloat16)
    return jnp.dot(hidden, down_mat, preferred_element_type=jnp.float32).astype(jnp.bfloat16)

def moe_layer(arrays):
    tokens_in, gain_row, gate_mats, up_mats, down_mats, route_rows, mix_rows = arrays
    normed = rms_normed(tokens_in, gain_row)
    summed = tokens_in.astype(jnp.float32)
    capacity = N_EP * CAP
    places = jnp.arange(capacity, dtype=jnp.int32)
    for expert in range(N_EP // SLICES):
        chosen = route_rows == expert
        member = jnp.any(chosen, axis=-1)
        weight = lax.optimization_barrier(jnp.sum(jnp.where(chosen, mix_rows, jnp.zeros_like(mix_rows)), axis=-1))
        picked = jnp.nonzero(member, size=capacity, fill_value=0)[0].astype(jnp.int32)
        filled = places < jnp.sum(member.astype(jnp.int32))
        token_rows = normed[picked]
        output = jnp.zeros((capacity, D), jnp.float32)
        for slice_index in range(SLICES):
            column = expert * SLICES + slice_index
            partial_value = expert_block(token_rows, gate_mats[column], up_mats[column], down_mats[column])
            output = output + lax.optimization_barrier(partial_value).astype(jnp.float32)
        scaled = jnp.where(filled, weight[picked], jnp.zeros_like(weight[picked]))
        summed = summed.at[picked].add(scaled[:, None] * output)
    return summed.astype(jnp.bfloat16)

def reference(tokens, gain_section, gate_weight, up_weight, down_weight, routes, mixing):
    block_out = lax.map(moe_layer, (tokens, gain_section, gate_weight, up_weight, down_weight, routes, mixing))
    return jnp.roll(block_out, 1, axis=0)
```

```python
import functools

import jax
import jax.numpy as jnp
from jax import lax
from jax.experimental import pallas as pl
from jax.experimental.pallas import tpu as pltpu
from jax.sharding import PartitionSpec as P

CAP = 32
WAVE = 4
EPSILON = 1e-06
N_Y, N_Z, N_CORE = 8, 2, 2
BF16, F32 = jnp.bfloat16, jnp.float32
ROOM = 24 * 1024 * 1024
ORDER = (0, 1, 3, 2)
VMEM = pl.BlockSpec(memory_space=pltpu.VMEM)


def permuted(x, move, sections=1, by=0):
    pairs = []
    for sec in range(sections):
        for y in range(N_Y):
            for z in range(N_Z):
                for core in range(N_CORE):
                    y2, z2, core2 = move(y, z, core)
                    source = (y * N_Z + z) * N_CORE + core
                    target = ((y2 % N_Y) * N_Z + z2) * N_CORE + core2
                    lanes = N_Y * N_Z * N_CORE
                    pairs.append((sec * lanes + source, ((sec + by) % sections) * lanes + target))
    return lax.ppermute(x, "ep" if sections == 1 else ("pp", "ep"), pairs)


def other_core(x):
    return permuted(x, lambda y, z, core: (y, z, 1 - core))


def other_plane(x):
    return permuted(x, lambda y, z, core: (y, 1 - z, core))


def pair_swap(x):
    return permuted(x, lambda y, z, core: (y ^ 1, z, core))


def stay(y, z, core):
    return y, z, core


def exchanged(x, planes):
    groups = []
    for parity in range(2):
        for core in range(N_CORE):
            members = [
                [((2 * half + parity) * N_Z + z) * N_CORE + core for z in range(N_Z)]
                for half in range(WAVE)
            ]
            if planes == N_Z:
                groups.append(sum(members, []))
            else:
                groups += [[member[z] for member in members] for z in range(N_Z)]
    parts = x.reshape(len(groups[0]), -1, x.shape[-1])
    parts = lax.all_to_all(
        parts, "ep", split_axis=0, concat_axis=0, axis_index_groups=groups, tiled=True
    )
    return parts.reshape(x.shape)


def called(kernel, out_shape, flops, moved, *xs, scalars=0):
    return pl.pallas_call(
        kernel,
        out_shape=out_shape,
        in_specs=[pl.BlockSpec(memory_space=pltpu.SMEM)] * scalars + [VMEM] * (len(xs) - scalars),
        out_specs=jax.tree.map(lambda _: VMEM, out_shape),
        compiler_params=pltpu.CompilerParams(vmem_limit_bytes=ROOM),
        cost_estimate=pl.CostEstimate(flops=0, bytes_accessed=0, transcendentals=0),
    )(*xs)


def pack_kernel(expert_ref, tokens_ref, gain_ref, routes_ref, mixing_ref, packed_ref, weight_ref):
    widened = tokens_ref[...].astype(F32)
    scale = lax.rsqrt(jnp.mean(widened * widened, axis=-1, keepdims=True) + EPSILON)
    normed = (widened * scale * gain_ref[...].astype(F32)).astype(BF16)
    rows = tokens_ref.shape[0]
    shape = (WAVE * CAP, rows)
    row = lax.broadcasted_iota(jnp.int32, shape, 0)
    member = jnp.zeros(shape, F32)
    weight = jnp.zeros(shape, F32)
    for k in range(routes_ref.shape[0]):
        hit = routes_ref[k : k + 1, :] == row // CAP
        member = jnp.where(hit, 1.0, member)
        weight = weight + jnp.where(hit, mixing_ref[k : k + 1, :], 0.0)
    upto = lax.broadcasted_iota(jnp.int32, (rows, rows), 0) <= lax.broadcasted_iota(
        jnp.int32, (rows, rows), 1
    )
    count = jnp.dot(
        member.astype(BF16), jnp.where(upto, 1.0, 0.0).astype(BF16), preferred_element_type=F32
    )
    slot = (row % CAP + 1).astype(F32)
    onehot = jnp.where((count == slot) & (member > 0.0), 1.0, 0.0)
    weight = weight * onehot
    for at in range(WAVE):
        start = (at + WAVE - expert_ref[0]) % WAVE * CAP
        weight_ref[pl.ds(pl.multiple_of(start, CAP), CAP)] = weight[at * CAP : (at + 1) * CAP]
    packed_ref[...] = jnp.dot(
        onehot.astype(BF16), normed, preferred_element_type=F32
    ).astype(BF16)


def sort_kernel(expert_ref, held_ref, first_ref, last_ref, all_ref):
    for index, k in enumerate(ORDER):
        at = (expert_ref[0] + WAVE - k) % WAVE * CAP
        piece = held_ref[pl.ds(pl.multiple_of(at, CAP), CAP)]
        all_ref[index * CAP : (index + 1) * CAP] = piece
        part, start = ((first_ref, last_ref)[index // 2], index % 2 * CAP)
        part[start : start + CAP] = piece


def expert_kernel(spans, *refs):
    xs, mats, out_ref = refs[: len(spans)], refs[len(spans) : -1], refs[-1]
    rows = jnp.concatenate([x[at : at + n] for x, (at, n) in zip(xs, spans)], axis=0)
    across = (((1,), (1,)), ((), ()))
    total = None
    for gate, up, down in (mats[:3], mats[3:]):
        gate_proj = lax.dot_general(rows, gate[...], across, preferred_element_type=F32)
        up_proj = lax.dot_general(rows, up[...], across, preferred_element_type=F32)
        hidden = (jax.nn.silu(gate_proj) * up_proj).astype(BF16)
        part = jnp.dot(hidden, down[...], preferred_element_type=F32)
        total = part if total is None else total + part
    out_ref[...] = total.astype(out_ref.dtype)


def expert_rows(xs, mats, dtype, spans=None):
    spans = spans or tuple((0, x.shape[0]) for x in xs)
    rows = sum(n for _, n in spans)
    out = jax.ShapeDtypeStruct((rows, xs[0].shape[1]), dtype)
    kernel = functools.partial(expert_kernel, spans)
    return called(kernel, out, 2 * rows * 2048 * 1152, 6 << 20, *xs, *mats)


def add_kernel(at, near_at, size, mine_ref, *refs):
    adds, outs = refs[: len(near_at)], refs[len(near_at) :]
    for index, out in enumerate(outs):
        total = mine_ref[at + index * size : at + (index + 1) * size]
        for add, start in zip(adds, near_at):
            total = total + add[start + index * size : start + (index + 1) * size].astype(F32)
        out[...] = total.astype(BF16)


def added(mine, at, size, count, *adds):
    out = [jax.ShapeDtypeStruct((size, mine.shape[1]), BF16)] * count
    kernel = functools.partial(add_kernel, at, tuple(start for _, start in adds), size)
    return called(kernel, out, 1 << 18, 1 << 20, mine, *[add for add, _ in adds])


def combine_kernel(tokens_ref, weight_ref, *refs):
    pieces, out_ref = refs[:-1], refs[-1]
    weight = weight_ref[...].T
    high = weight.astype(BF16)
    rest = weight - high.astype(F32)
    middle = rest.astype(BF16)
    low = (rest - middle.astype(F32)).astype(BF16)
    rows = jnp.concatenate([piece[...] for piece in pieces], axis=0)
    total = jnp.dot(
        jnp.concatenate([high, middle], axis=1),
        jnp.concatenate([rows, rows], axis=0),
        preferred_element_type=F32,
    )
    total = total + jnp.dot(low, rows, preferred_element_type=F32)
    out_ref[...] = (tokens_ref[...].astype(F32) + total).astype(BF16)


def tied(*xs):
    return lax.optimization_barrier(xs)


def body(sections, tokens, gain, gate, up, down, routes, mixing):
    tokens, gate, up, down = tokens[0], gate[0, 0].T, up[0, 0].T, down[0, 0]
    rows, features = tokens.shape
    slots, half = WAVE * CAP, 2 * CAP
    expert = (lax.axis_index("ep") // (2 * N_Z * N_CORE)).astype(jnp.int32).reshape(1)

    packed, weight = called(
        pack_kernel,
        [
            jax.ShapeDtypeStruct((slots, features), BF16),
            jax.ShapeDtypeStruct((slots, rows), F32),
        ],
        2 * slots * rows * features,
        2 << 20,
        expert,
        tokens,
        gain,
        routes[0].T,
        mixing[0].T,
        scalars=1,
    )

    held, before, *mats = tied(
        exchanged(packed, 1),
        permuted(tokens, stay, sections, 1),
        other_core(gate),
        other_core(up),
        other_core(down),
    )
    mats = (gate, up, down, *mats)
    quarter = jax.ShapeDtypeStruct((half, features), BF16)
    held_a, held_b, held = called(
        sort_kernel,
        [quarter, quarter, jax.ShapeDtypeStruct((slots, features), BF16)],
        0,
        1 << 20,
        expert,
        held,
        scalars=1,
    )
    crossed_a, crossed_b = other_plane(held_a), other_plane(held_b)
    twin_a = pair_swap(crossed_a)
    sent = expert_rows([pair_swap(held)], mats, BF16)
    crossed_b, twin_a, sent, weight = tied(crossed_b, twin_a, sent, weight)
    twin_b = pair_swap(crossed_b)
    weight = permuted(weight, stay, sections, 1)
    theirs_a, sent = tied(pair_swap(expert_rows([twin_a], mats, BF16)), sent)
    theirs = pair_swap(sent)
    mine = expert_rows([crossed_a, crossed_b, held], mats, F32)
    mine, twin_b = tied(mine, twin_b)
    theirs_b = pair_swap(expert_rows([twin_b], mats, BF16))

    (far_a,) = added(mine, 0, half, 1, (theirs_a, 0))
    (far_b,) = added(mine, half, half, 1, (theirs_b, 0))
    pieces = added(mine, 2 * half, CAP, 2, (theirs, 0), (other_plane(far_a), 0))
    pieces += added(mine, 3 * half, CAP, 2, (theirs, half), (other_plane(far_b), 0))
    back = {
        k: permuted(piece, lambda y, z, core, k=k: (y - 2 * k, z, core), sections, 1)
        for k, piece in zip(ORDER, pieces)
    }
    return called(
        combine_kernel,
        jax.ShapeDtypeStruct((rows, features), BF16),
        6 * rows * slots * features,
        3 << 20,
        before,
        weight,
        *[back[k] for k in range(WAVE)],
    )[None]


def solution(mesh):
    placed = (
        P("pp", "ep", None),
        P("pp", None),
        P("pp", "ep", None, None),
        P("pp", "ep", None, None),
        P("pp", "ep", None, None),
        P("pp", "ep", None),
        P("pp", "ep", None),
    )
    return jax.shard_map(
        functools.partial(body, mesh.shape["pp"]),
        mesh=mesh,
        in_specs=placed,
        out_specs=P("pp", "ep", None),
        check_vma=False,
    )
```

```python
import functools

import jax
import jax.numpy as jnp
from jax import lax
from jax.experimental import pallas as pl
from jax.experimental.pallas import tpu as pltpu
from jax.sharding import PartitionSpec as P

CAP = 32
WAVE = 4
EPSILON = 1e-06
N_Y, N_Z, N_CORE = 8, 2, 2
BF16, F32 = jnp.bfloat16, jnp.float32
ROOM = 24 * 1024 * 1024
ORDER = (0, 1, 3, 2)
VMEM = pl.BlockSpec(memory_space=pltpu.VMEM)


def permuted(x, move, sections=1, by=0):
    pairs = []
    for sec in range(sections):
        for y in range(N_Y):
            for z in range(N_Z):
                for core in range(N_CORE):
                    y2, z2, core2 = move(y, z, core)
                    source = (y * N_Z + z) * N_CORE + core
                    target = ((y2 % N_Y) * N_Z + z2) * N_CORE + core2
                    lanes = N_Y * N_Z * N_CORE
                    pairs.append((sec * lanes + source, ((sec + by) % sections) * lanes + target))
    return lax.ppermute(x, "ep" if sections == 1 else ("pp", "ep"), pairs)


def other_core(x):
    return permuted(x, lambda y, z, core: (y, z, 1 - core))


def other_plane(x):
    return permuted(x, lambda y, z, core: (y, 1 - z, core))


def pair_swap(x):
    return permuted(x, lambda y, z, core: (y ^ 1, z, core))


def stay(y, z, core):
    return y, z, core


def exchanged(x, planes):
    groups = []
    for parity in range(2):
        for core in range(N_CORE):
            members = [
                [((2 * half + parity) * N_Z + z) * N_CORE + core for z in range(N_Z)]
                for half in range(WAVE)
            ]
            if planes == N_Z:
                groups.append(sum(members, []))
            else:
                groups += [[member[z] for member in members] for z in range(N_Z)]
    parts = x.reshape(len(groups[0]), -1, x.shape[-1])
    parts = lax.all_to_all(
        parts, "ep", split_axis=0, concat_axis=0, axis_index_groups=groups, tiled=True
    )
    return parts.reshape(x.shape)


def called(kernel, out_shape, *xs, scalars=0):
    return pl.pallas_call(
        kernel,
        out_shape=out_shape,
        in_specs=[pl.BlockSpec(memory_space=pltpu.SMEM)] * scalars + [VMEM] * (len(xs) - scalars),
        out_specs=jax.tree.map(lambda _: VMEM, out_shape),
        compiler_params=pltpu.CompilerParams(vmem_limit_bytes=ROOM),
        cost_estimate=pl.CostEstimate(flops=0, bytes_accessed=0, transcendentals=0),
    )(*xs)


def pack_kernel(place_ref, tokens_ref, gain_ref, routes_ref, mixing_ref, packed_ref, weight_ref):
    widened = tokens_ref[...].astype(F32)
    scale = lax.rsqrt(jnp.mean(widened * widened, axis=-1, keepdims=True) + EPSILON)
    normed = (widened * scale * gain_ref[...].astype(F32)).astype(BF16)
    rows = tokens_ref.shape[0]
    shape = (WAVE * CAP, rows)
    row = lax.broadcasted_iota(jnp.int32, shape, 0)
    member = jnp.zeros(shape, F32)
    weight = jnp.zeros(shape, F32)
    for k in range(routes_ref.shape[0]):
        hit = routes_ref[k : k + 1, :] == row // CAP
        member = jnp.where(hit, 1.0, member)
        weight = weight + jnp.where(hit, mixing_ref[k : k + 1, :], 0.0)
    upto = lax.broadcasted_iota(jnp.int32, (rows, rows), 0) <= lax.broadcasted_iota(
        jnp.int32, (rows, rows), 1
    )
    count = jnp.dot(
        member.astype(BF16), jnp.where(upto, 1.0, 0.0).astype(BF16), preferred_element_type=F32
    )
    slot = (row % CAP + 1).astype(F32)
    onehot = jnp.where((count == slot) & (member > 0.0), 1.0, 0.0)
    weight = weight * onehot
    for at in range(WAVE):
        start = (at + WAVE - place_ref[0]) % WAVE * CAP
        weight_ref[pl.ds(pl.multiple_of(start, CAP), CAP)] = weight[at * CAP : (at + 1) * CAP]
    packed = jnp.dot(onehot.astype(BF16), normed, preferred_element_type=F32).astype(BF16)
    for at in range(N_Z * WAVE):
        chunk = at // N_Z * CAP
        packed_ref[at * CAP : (at + 1) * CAP] = packed[chunk : chunk + CAP]


def stack_kernel(*refs):
    count = len(refs) // 3
    for index, out in enumerate(refs[2 * count :]):
        rows = refs[2 * index].shape[0]
        out[:rows] = refs[2 * index][...]
        out[rows:] = refs[2 * index + 1][...]


def sort_kernel(place_ref, held_ref, far_ref, near_ref):
    for other, out_ref in ((1, far_ref), (0, near_ref)):
        plane = (place_ref[1] + other) % N_Z
        for index, k in enumerate(ORDER):
            at = ((place_ref[0] + WAVE - k) % WAVE * N_Z + plane) * CAP
            out_ref[index * CAP : (index + 1) * CAP] = held_ref[pl.ds(pl.multiple_of(at, CAP), CAP)]


def hidden_rows(rows, gates, ups):
    across = (((1,), (1,)), ((), ()))
    gate_proj = lax.dot_general(rows, gates[...], across, preferred_element_type=F32)
    up_proj = lax.dot_general(rows, ups[...], across, preferred_element_type=F32)
    return (jax.nn.silu(gate_proj) * up_proj).astype(BF16)


def hidden_kernel(rows_ref, gates, ups, out_ref):
    out_ref[...] = hidden_rows(rows_ref[...], gates, ups)


def mine_kernel(far_ref, near_ref, gates, ups, downs, out_ref):
    rows = jnp.concatenate([far_ref[...], near_ref[...]], axis=0)
    hidden = hidden_rows(rows, gates, ups)
    out_ref[...] = jnp.dot(hidden, downs[...], preferred_element_type=F32)


def sum_kernel(at, hidden_at, mine_ref, hidden_ref, downs, *refs):
    adds, outs = (refs[:1], refs[1:]) if len(refs) == 3 else ((), refs)
    size = sum(out.shape[0] for out in outs)
    total = mine_ref[at : at + size] + jnp.dot(
        hidden_ref[hidden_at : hidden_at + size], downs[...], preferred_element_type=F32
    )
    for add in adds:
        total = total + add[...].astype(F32)
    start = 0
    for out in outs:
        out[...] = total[start : start + out.shape[0]].astype(BF16)
        start += out.shape[0]


def summed(at, hidden_at, size, mine, hidden, downs, *far):
    out = [jax.ShapeDtypeStruct((size, mine.shape[1]), BF16)] * 2
    kernel = functools.partial(sum_kernel, at, hidden_at)
    return called(kernel, out, mine, hidden, downs, *far)


def combine_kernel(tokens_ref, weight_ref, *refs):
    pieces, out_ref = refs[:-1], refs[-1]
    weight = weight_ref[...].T
    high = weight.astype(BF16)
    rest = weight - high.astype(F32)
    middle = rest.astype(BF16)
    low = (rest - middle.astype(F32)).astype(BF16)
    rows = jnp.concatenate([piece[...] for piece in pieces], axis=0)
    total = jnp.dot(
        jnp.concatenate([high, middle], axis=1),
        jnp.concatenate([rows, rows], axis=0),
        preferred_element_type=F32,
    )
    total = total + jnp.dot(low, rows, preferred_element_type=F32)
    out_ref[...] = (tokens_ref[...].astype(F32) + total).astype(BF16)


def tied(*xs):
    return lax.optimization_barrier(xs)


def body(sections, tokens, gain, gate, up, down, routes, mixing):
    tokens, gate, up, down = tokens[0], gate[0, 0].T, up[0, 0].T, down[0, 0]
    rows, features = tokens.shape
    slots, half = WAVE * CAP, 2 * CAP
    ep = lax.axis_index("ep").astype(jnp.int32)
    place = jnp.stack([ep // (2 * N_Z * N_CORE), ep // N_CORE % N_Z])

    packed, weight = called(
        pack_kernel,
        [
            jax.ShapeDtypeStruct((N_Z * slots, features), BF16),
            jax.ShapeDtypeStruct((slots, rows), F32),
        ],
        place,
        tokens,
        gain,
        routes[0].T,
        mixing[0].T,
        scalars=1,
    )

    pairs = ((gate, other_core(gate)), (up, other_core(up)), (down, other_core(down)))
    stack = jax.ShapeDtypeStruct((2 * up.shape[0], features), BF16)
    held, weight, gates, ups, downs = tied(
        exchanged(packed, N_Z),
        permuted(weight, stay, sections, 1),
        *called(stack_kernel, [stack] * 3, *[mat for both in pairs for mat in both]),
    )
    twin_down = pair_swap(down)

    half_rows = jax.ShapeDtypeStruct((slots, features), BF16)
    far, near = called(sort_kernel, [half_rows, half_rows], place, held, scalars=1)
    far, near, tokens = tied(far, near, tokens)
    before = permuted(tokens, stay, sections, 1)
    sums = jax.ShapeDtypeStruct((N_Z * slots, features), F32)
    mine = called(mine_kernel, sums, far, near, gates, ups, downs)
    mine, twin_far, twin_down = tied(mine, pair_swap(far), twin_down)
    (twin_downs,) = called(stack_kernel, [stack], twin_down, other_core(twin_down))
    units = jax.ShapeDtypeStruct((slots, stack.shape[0]), BF16)
    hidden_far = pair_swap(called(hidden_kernel, units, twin_far, gates, ups))
    hidden_far, near, before, twin_downs = tied(hidden_far, near, before, twin_downs)
    hidden_near = pair_swap(called(hidden_kernel, units, pair_swap(near), gates, ups))

    crossing = summed(0, 0, half, mine, hidden_far, twin_downs)
    pieces = []
    for index, part in enumerate(crossing):
        at = index * half
        pieces += summed(
            slots + at, at, CAP, mine, hidden_near, twin_downs, other_plane(part)
        )
    back = {
        k: permuted(piece, lambda y, z, core, k=k: (y - 2 * k, z, core), sections, 1)
        for k, piece in zip(ORDER, pieces)
    }
    return called(
        combine_kernel,
        jax.ShapeDtypeStruct((rows, features), BF16),
        before,
        weight,
        *[back[k] for k in range(WAVE)],
    )[None]


def solution(mesh):
    placed = (
        P("pp", "ep", None),
        P("pp", None),
        P("pp", "ep", None, None),
        P("pp", "ep", None, None),
        P("pp", "ep", None, None),
        P("pp", "ep", None),
        P("pp", "ep", None),
    )
    return jax.shard_map(
        functools.partial(body, mesh.shape["pp"]),
        mesh=mesh,
        in_specs=placed,
        out_specs=P("pp", "ep", None),
        check_vma=False,
    )
```

```python
import functools

import jax
import jax.numpy as jnp
from jax import lax
from jax.experimental import pallas as pl
from jax.experimental.pallas import tpu as pltpu
from jax.sharding import PartitionSpec as P

CAP = 32
WAVE = 4
EPSILON = 1e-06
N_Y, N_Z, N_CORE = 8, 2, 2
BF16, F32 = jnp.bfloat16, jnp.float32
ROOM = 24 * 1024 * 1024
ORDER = (0, 1, 3, 2)
VMEM = pl.BlockSpec(memory_space=pltpu.VMEM)


def permuted(x, move, sections=1, by=0):
    pairs = []
    for sec in range(sections):
        for y in range(N_Y):
            for z in range(N_Z):
                for core in range(N_CORE):
                    y2, z2, core2 = move(y, z, core)
                    source = (y * N_Z + z) * N_CORE + core
                    target = ((y2 % N_Y) * N_Z + z2) * N_CORE + core2
                    lanes = N_Y * N_Z * N_CORE
                    pairs.append((sec * lanes + source, ((sec + by) % sections) * lanes + target))
    return lax.ppermute(x, "ep" if sections == 1 else ("pp", "ep"), pairs)


def other_core(x):
    return permuted(x, lambda y, z, core: (y, z, 1 - core))


def other_plane(x):
    return permuted(x, lambda y, z, core: (y, 1 - z, core))


def pair_swap(x):
    return permuted(x, lambda y, z, core: (y ^ 1, z, core))


def stay(y, z, core):
    return y, z, core


def exchanged(x, planes):
    groups = []
    for parity in range(2):
        for core in range(N_CORE):
            members = [
                [((2 * half + parity) * N_Z + z) * N_CORE + core for z in range(N_Z)]
                for half in range(WAVE)
            ]
            if planes == N_Z:
                groups.append(sum(members, []))
            else:
                groups += [[member[z] for member in members] for z in range(N_Z)]
    parts = x.reshape(len(groups[0]), -1, x.shape[-1])
    parts = lax.all_to_all(
        parts, "ep", split_axis=0, concat_axis=0, axis_index_groups=groups, tiled=True
    )
    return parts.reshape(x.shape)


def called(kernel, out_shape, *xs, scalars=0, room=ROOM):
    return pl.pallas_call(
        kernel,
        out_shape=out_shape,
        in_specs=[pl.BlockSpec(memory_space=pltpu.SMEM)] * scalars + [VMEM] * (len(xs) - scalars),
        out_specs=jax.tree.map(lambda _: VMEM, out_shape),
        compiler_params=pltpu.CompilerParams(vmem_limit_bytes=room),
        cost_estimate=pl.CostEstimate(flops=0, bytes_accessed=0, transcendentals=0),
    )(*xs)


def pack_kernel(place_ref, tokens_ref, gain_ref, routes_ref, mixing_ref, packed_ref, weight_ref):
    widened = tokens_ref[...].astype(F32)
    scale = lax.rsqrt(jnp.mean(widened * widened, axis=-1, keepdims=True) + EPSILON)
    normed = (widened * scale * gain_ref[...].astype(F32)).astype(BF16)
    rows = tokens_ref.shape[0]
    shape = (WAVE * CAP, rows)
    row = lax.broadcasted_iota(jnp.int32, shape, 0)
    member = jnp.zeros(shape, F32)
    weight = jnp.zeros(shape, F32)
    for k in range(routes_ref.shape[0]):
        hit = routes_ref[k : k + 1, :] == row // CAP
        member = jnp.where(hit, 1.0, member)
        weight = weight + jnp.where(hit, mixing_ref[k : k + 1, :], 0.0)
    upto = lax.broadcasted_iota(jnp.int32, (rows, rows), 0) <= lax.broadcasted_iota(
        jnp.int32, (rows, rows), 1
    )
    count = jnp.dot(
        member.astype(BF16), jnp.where(upto, 1.0, 0.0).astype(BF16), preferred_element_type=F32
    )
    slot = (row % CAP + 1).astype(F32)
    onehot = jnp.where((count == slot) & (member > 0.0), 1.0, 0.0)
    weight = weight * onehot
    for at in range(WAVE):
        start = (at + WAVE - place_ref[0]) % WAVE * CAP
        weight_ref[pl.ds(pl.multiple_of(start, CAP), CAP)] = weight[at * CAP : (at + 1) * CAP]
    packed = jnp.dot(onehot.astype(BF16), normed, preferred_element_type=F32).astype(BF16)
    for at in range(N_Z * WAVE):
        chunk = at // N_Z * CAP
        packed_ref[at * CAP : (at + 1) * CAP] = packed[chunk : chunk + CAP]


def stack_kernel(*refs):
    count = len(refs) // 3
    for index, out in enumerate(refs[2 * count :]):
        rows = refs[2 * index].shape[0]
        out[:rows] = refs[2 * index][...]
        out[rows:] = refs[2 * index + 1][...]


def sort_kernel(place_ref, held_ref, far_ref, near_ref):
    for other, out_ref in ((1, far_ref), (0, near_ref)):
        plane = (place_ref[1] + other) % N_Z
        for index, k in enumerate(ORDER):
            at = ((place_ref[0] + WAVE - k) % WAVE * N_Z + plane) * CAP
            out_ref[index * CAP : (index + 1) * CAP] = held_ref[pl.ds(pl.multiple_of(at, CAP), CAP)]


def hidden_rows(rows, gates, ups):
    across = (((1,), (1,)), ((), ()))
    gate_proj = lax.dot_general(rows, gates[...], across, preferred_element_type=F32)
    up_proj = lax.dot_general(rows, ups[...], across, preferred_element_type=F32)
    return (jax.nn.silu(gate_proj) * up_proj).astype(BF16)


def hidden_kernel(rows_ref, gates, ups, out_ref):
    out_ref[...] = hidden_rows(rows_ref[...], gates, ups)


def mine_kernel(far_ref, near_ref, gates, ups, downs, out_ref):
    rows = jnp.concatenate([far_ref[...], near_ref[...]], axis=0)
    hidden = hidden_rows(rows, gates, ups)
    out_ref[...] = jnp.dot(hidden, downs[...], preferred_element_type=F32)


def sum_kernel(at, hidden_at, mine_ref, hidden_ref, downs, *refs):
    adds, outs = (refs[:1], refs[1:]) if len(refs) == 3 else ((), refs)
    size = sum(out.shape[0] for out in outs)
    total = mine_ref[at : at + size] + jnp.dot(
        hidden_ref[hidden_at : hidden_at + size], downs[...], preferred_element_type=F32
    )
    for add in adds:
        total = total + add[...].astype(F32)
    start = 0
    for out in outs:
        out[...] = total[start : start + out.shape[0]].astype(BF16)
        start += out.shape[0]


def summed(at, hidden_at, size, mine, hidden, downs, *far):
    out = [jax.ShapeDtypeStruct((size, mine.shape[1]), BF16)] * 2
    kernel = functools.partial(sum_kernel, at, hidden_at)
    return called(kernel, out, mine, hidden, downs, *far)


def combine_kernel(tokens_ref, weight_ref, *refs):
    pieces, out_ref = refs[:-1], refs[-1]
    weight = weight_ref[...].T
    high = weight.astype(BF16)
    rest = weight - high.astype(F32)
    middle = rest.astype(BF16)
    low = (rest - middle.astype(F32)).astype(BF16)
    rows = jnp.concatenate([piece[...] for piece in pieces], axis=0)
    total = jnp.dot(
        jnp.concatenate([high, middle], axis=1),
        jnp.concatenate([rows, rows], axis=0),
        preferred_element_type=F32,
    )
    total = total + jnp.dot(low, rows, preferred_element_type=F32)
    out_ref[...] = (tokens_ref[...].astype(F32) + total).astype(BF16)


def tied(*xs):
    return lax.optimization_barrier(xs)


def body(sections, tokens, gain, gate, up, down, routes, mixing):
    tokens, gate, up, down = tokens[0], gate[0, 0].T, up[0, 0].T, down[0, 0]
    rows, features = tokens.shape
    slots, half = WAVE * CAP, 2 * CAP
    ep = lax.axis_index("ep").astype(jnp.int32)
    place = jnp.stack([ep // (2 * N_Z * N_CORE), ep // N_CORE % N_Z])

    packed, weight = called(
        pack_kernel,
        [
            jax.ShapeDtypeStruct((N_Z * slots, features), BF16),
            jax.ShapeDtypeStruct((slots, rows), F32),
        ],
        place,
        tokens,
        gain,
        routes[0].T,
        mixing[0].T,
        scalars=1,
        room=60 * 1024 * 1024,
    )

    pairs = ((gate, other_core(gate)), (up, other_core(up)), (down, other_core(down)))
    stack = jax.ShapeDtypeStruct((2 * up.shape[0], features), BF16)
    held, weight, gates, ups, downs = tied(
        exchanged(packed, N_Z),
        permuted(weight, stay, sections, 1),
        *called(stack_kernel, [stack] * 3, *[mat for both in pairs for mat in both]),
    )
    twin_down = pair_swap(down)

    half_rows = jax.ShapeDtypeStruct((slots, features), BF16)
    far, near = called(sort_kernel, [half_rows, half_rows], place, held, scalars=1)
    far, near, tokens = tied(far, near, tokens)
    before = permuted(tokens, stay, sections, 1)
    sums = jax.ShapeDtypeStruct((N_Z * slots, features), F32)
    mine = called(mine_kernel, sums, far, near, gates, ups, downs)
    mine, twin_far, twin_down = tied(mine, pair_swap(far), twin_down)
    (twin_downs,) = called(stack_kernel, [stack], twin_down, other_core(twin_down))
    units = jax.ShapeDtypeStruct((slots, stack.shape[0]), BF16)
    hidden_far = pair_swap(called(hidden_kernel, units, twin_far, gates, ups))
    hidden_far, near, before, twin_downs = tied(hidden_far, near, before, twin_downs)
    hidden_near = pair_swap(called(hidden_kernel, units, pair_swap(near), gates, ups))

    crossing = summed(0, 0, half, mine, hidden_far, twin_downs)
    pieces = []
    for index, part in enumerate(crossing):
        at = index * half
        pieces += summed(
            slots + at, at, CAP, mine, hidden_near, twin_downs, other_plane(part)
        )
    back = {
        k: permuted(piece, lambda y, z, core, k=k: (y - 2 * k, z, core), sections, 1)
        for k, piece in zip(ORDER, pieces)
    }
    return called(
        combine_kernel,
        jax.ShapeDtypeStruct((rows, features), BF16),
        before,
        weight,
        *[back[k] for k in range(WAVE)],
    )[None]


def solution(mesh):
    placed = (
        P("pp", "ep", None),
        P("pp", None),
        P("pp", "ep", None, None),
        P("pp", "ep", None, None),
        P("pp", "ep", None, None),
        P("pp", "ep", None),
        P("pp", "ep", None),
    )
    return jax.shard_map(
        functools.partial(body, mesh.shape["pp"]),
        mesh=mesh,
        in_specs=placed,
        out_specs=P("pp", "ep", None),
        check_vma=False,
    )
```
